256 devices in a mesh: sample: 16 (over x, y), landmark: 16 (over z, core).
Axes of the slice: x: 4, y: 4, z: 8, core: 2. Of those that a mesh axis runs over, the one named last changes fastest.
Arguments:
- embeddings: float32 [65536, 512], P('sample')
- landmark_index: int32 [8192], P('landmark'), may hold values from 0 to 65535, as said below
- cluster_weights: float32 [8192, 256], P('landmark'), may hold values from -6 to 6
Outputs:
- scores: float32 [65536, 256], P(('sample', 'landmark'))
The draws below stay inside these ranges and needn't reach their ends.
Inputs may be any that keep to these rules, and one draw needn't show every extreme that they name: `landmark_index`: 8192 distinct sample indices; 0 and 65535 are always among them.
All inputs are finite; a program needn't handle non-finite values.
Results may differ from the reference program's by a relative error of at most 0.00018.
Values sent between devices are 32-bit elements; how exact they have to be, the bound alone decides.
A program may use at most 128 MiB of HBM per device.

```python
import math
import jax
import jax.numpy as jnp
from jax import lax

D = 512
C = 256
M = 8192
ROWS_DEV = 4096
NS = 65536


def draw_embeddings(key, part):
    key_label = jax.random.fold_in(key, 12)
    key_noise = jax.random.fold_in(key, 13)
    key_scale = jax.random.fold_in(key, 14)
    far_rows = jax.random.randint(key_label, (NS,), 0, 16) == 0
    noise = jnp.clip(jax.random.normal(key_noise, (NS, D), jnp.float32), -3.5, 3.5)
    far_scale = jnp.exp(jax.random.uniform(key_scale, (NS,), jnp.float32, math.log(4.0), math.log(12.0)))
    scales = jnp.where(far_rows, far_scale, 3.2)
    mixed = 0.6 * noise / math.sqrt(D)
    return (scales[:, None] * mixed).astype(jnp.float32)


def draw_landmark_index(key, part):
    inner = jax.random.permutation(jax.random.fold_in(key, 21), NS - 2)[:M - 2] + 1
    ends = jnp.array([0, NS - 1], jnp.int32)
    full = jnp.concatenate([ends, inner.astype(jnp.int32)])
    return jax.random.permutation(jax.random.fold_in(key, 22), full).astype(jnp.int32)


def block_scale(stream_key, dims, pieces, smallest, largest):
    level, own = 1.0, jax.random.fold_in(stream_key, 6)
    for position, blocks in pieces:
        heights = jnp.exp(jax.random.uniform(jax.random.fold_in(own, position), (blocks,), jnp.float32, smallest / len(pieces), largest / len(pieces)))
        level = level * jnp.repeat(heights, dims[position] // blocks).reshape([-1 if axis == position else 1 for axis in range(len(dims))])
    return level


def gaussian(key, dims, deviation, reach, pieces=(), kind=jnp.bfloat16):
    drawn = deviation * jax.random.normal(key, dims, jnp.float32)
    if pieces:
        drawn = drawn * block_scale(key, dims, pieces, -0.22, 0.18)
    return jnp.clip(drawn, -reach, reach).astype(kind)


def setup_inputs(seed: int = 0) -> dict:
    seeds = jax.random.split(jax.random.key(seed), 4)
    embeddings = draw_embeddings(jax.random.fold_in(seeds[3], 71), 0)
    landmark_index = draw_landmark_index(jax.random.fold_in(seeds[3], 71), 0)
    cluster_weights = gaussian(seeds[2], (M, C), 1.0, 6.0, ((0, 16),), jnp.float32)
    return dict(embeddings=embeddings, landmark_index=landmark_index, cluster_weights=cluster_weights)


kernel_gamma = 2.0


def reference(embeddings, landmark_index, cluster_weights):
    landmarks = jnp.take(embeddings, landmark_index.astype(jnp.int32), axis=0)
    land_sq = jnp.sum(landmarks * landmarks, axis=1)

    def score_block(row_block):
        row_sq = jnp.sum(row_block * row_block, axis=1)
        inner_prod = jnp.dot(row_block, landmarks.T, precision=lax.Precision.HIGHEST, preferred_element_type=jnp.float32)
        logits = (2.0 * inner_prod - row_sq[:, None] - land_sq[None, :]) * kernel_gamma
        row_max = jnp.max(logits, axis=1)
        kernel = jnp.exp(logits - row_max[:, None])
        weighted = jnp.dot(kernel, cluster_weights, precision=lax.Precision.HIGHEST, preferred_element_type=jnp.float32)
        return weighted / jnp.sum(kernel, axis=1)[:, None]

    row_blocks = embeddings.reshape(NS // ROWS_DEV, ROWS_DEV, D)
    return lax.map(score_block, row_blocks).reshape(NS, C)
```

```python
import jax
import jax.numpy as jnp
from jax import lax
from jax.sharding import PartitionSpec as P

kernel_gamma = 2.0


def dot3(a, b):
    return jnp.dot(a, b, precision=lax.Precision.HIGH, preferred_element_type=jnp.float32)


def shards(embeddings, landmark_index, cluster_weights):
    row_count = embeddings.shape[0]
    sample_pos = lax.axis_index("sample")
    offsets = landmark_index - sample_pos * row_count
    owned_mask = (offsets >= 0) & (offsets < row_count)
    picked = jnp.take(embeddings, jnp.clip(offsets, 0, row_count - 1), axis=0)
    picked = jnp.where(owned_mask[:, None], picked, 0.0)
    landmarks = lax.psum(picked, "sample")
    row_sq = jnp.sum(embeddings * embeddings, axis=1)
    land_sq = jnp.sum(landmarks * landmarks, axis=1)
    inner = dot3(embeddings, landmarks.T)
    logits = (2.0 * inner - row_sq[:, None] - land_sq[None, :]) * kernel_gamma
    top = lax.pmax(jnp.max(logits, axis=1), "landmark")
    kernel = jnp.exp(logits - top[:, None])
    mass = lax.psum_scatter(jnp.sum(kernel, axis=1), "landmark", tiled=True)
    weighted = lax.psum_scatter(dot3(kernel, cluster_weights), "landmark", tiled=True)
    return weighted / mass[:, None]


def solution(mesh):
    return jax.shard_map(
        shards,
        mesh=mesh,
        in_specs=(P("sample", None), P("landmark"), P("landmark", None)),
        out_specs=P(("sample", "landmark"), None),
        check_vma=False,
    )
```

```python
import jax
import jax.numpy as jnp
from jax import lax
from jax.experimental import pallas as pl
from jax.experimental.pallas import tpu as pltpu
from jax.sharding import PartitionSpec as P

MESH = pl.DeviceIdType.MESH
F32 = jnp.float32
BF16 = jnp.bfloat16

D = 512
C = 256
ROWS = 4096
OWN = 512
PAIR = 2 * OWN
RING = 8
CHUNK = 256
HALF = CHUNK // 2
STREAMS = 8
R = OWN // STREAMS
MSG = C + 8
LOADS = 8


def split(a):
    hi = a.astype(BF16)
    return hi, (a - hi.astype(F32)).astype(BF16)


def kernel(
    emb_hbm, idx_ref, w_hbm, out_ref,
    emb, pick, land, buf0, buf1, buf2, buf3, acc1, acc2, acc3,
    wts, ww, ll, lsq2, xx, xsq2, sent, got,
    load_sem, w_sem, send_sem, recv_sem, sib_send, sib_recv, ws_send, ws_recv, ring_send, ring_recv,
):
    sample = lax.axis_index("sample")
    mark = lax.axis_index("landmark")
    x, y = sample // 4, sample % 4
    z, core = mark // 2, mark % 2

    partners = [
        ((x + 1 - 2 * (x % 2)) * 4 + y, mark),
        ((3 - x) * 4 + y, mark),
        (x * 4 + y + 1 - 2 * (y % 2), mark),
        (x * 4 + 3 - y, mark),
    ]
    bits = [(x % 2 + x // 2) % 2, x // 2, (y % 2 + y // 2) % 2, y // 2]
    sibling = (sample, z * 2 + 1 - core)
    above = (sample, ((z + 1) % RING) * 2 + core)
    below = (sample, ((z + RING - 1) % RING) * 2 + core)

    loads = []
    for i in range(LOADS):
        part = pl.ds(i * (ROWS // LOADS), ROWS // LOADS)
        load = pltpu.make_async_copy(emb_hbm.at[part], emb.at[part], load_sem.at[i])
        load.start()
        loads.append(load)
    own_w = pl.ds(pl.multiple_of(core * OWN, OWN), OWN)
    w_load = pltpu.make_async_copy(w_hbm, wts.at[own_w], w_sem)
    w_load.start()

    barrier = pltpu.get_barrier_semaphore()
    for other in partners + [sibling, above, below]:
        pl.semaphore_signal(barrier, inc=1, device_id=other, device_id_type=MESH)
    pl.semaphore_wait(barrier, 7)

    w_load.wait()
    w_send = pltpu.make_async_remote_copy(
        wts.at[own_w], wts.at[own_w], ws_send, ws_recv, device_id=sibling, device_id_type=MESH
    )
    w_send.start()

    for load in loads:
        load.wait()

    first = sample * ROWS

    def pick_rows(i, carry):
        for u in range(16):
            row = i * 16 + u
            place = idx_ref[row] - first
            owned = jnp.logical_and(place >= 0, place < ROWS)
            found = emb[pl.ds(jnp.clip(place, 0, ROWS - 1), 1), :]
            pick[pl.ds(row, 1), :] = jnp.where(owned, found, 0.0)
        return carry

    def prepare(t):
        up = ((z + 2 * RING - 1 - t) % RING * 2 + core) * CHUNK
        down = ((z + 1 + t) % RING * 2 + core) * CHUNK + HALF
        for side, start in enumerate((up, down)):
            rows = emb[pl.ds(pl.multiple_of(start, HALF), HALF), :]
            hi, lo = split(4.0 * rows)
            here = pl.ds(side * HALF, HALF)
            xx[t, here, 0:D] = hi
            xx[t, here, D : 2 * D] = lo
            xx[t, here, 2 * D :] = hi
            sq = rows * rows
            sq = (sq[:, 0:128] + sq[:, 128:256]) + (sq[:, 256:384] + sq[:, 384:512])
            xsq2[t, :, side * HALF : (side + 1) * HALF] = 2.0 * jnp.sum(sq.T, axis=0, keepdims=True)

    def prepare_landmarks(start, count):
        here = pl.ds(pl.multiple_of(start, 16), count)
        rows = land[here, :]
        hi, lo = split(rows)
        ll[here, 0:D] = hi
        ll[here, D : 2 * D] = hi
        ll[here, 2 * D :] = lo
        lsq2[here, :] = jnp.broadcast_to(2.0 * jnp.sum(rows * rows, axis=1, keepdims=True), (count, 128))

    def prepare_weights():
        for g in range(PAIR // 256):
            hi, lo = split(wts[g * 256 : (g + 1) * 256, :].T)
            ww[0:C, g * 256 : (g + 1) * 256] = hi
            ww[C:, g * 256 : (g + 1) * 256] = lo

    lax.fori_loop(0, OWN // 16, pick_rows, 0)

    copies = []

    def send(step, j, src, dst, dim):
        copy = pltpu.make_async_remote_copy(
            src, dst, send_sem.at[step, j], recv_sem.at[step, j],
            device_id=partners[dim], device_id_type=MESH,
        )
        copy.start()
        copies.append(copy)
        return copy

    def rows_at(start, count):
        return pl.ds(pl.multiple_of(start, 8), count)

    flight = []
    for j in range(STREAMS):
        b0 = bits[j % 4]
        flight.append(send(0, j, pick.at[rows_at(j * R + (1 - b0) * (R // 2), R // 2)], buf0.at[j], j % 4))
    prepare(0)
    prepare(1)
    for j in range(STREAMS):
        b0, b1 = bits[j % 4], bits[(j + 1) % 4]
        flight[j].wait_recv()
        acc1[j] = pick[rows_at(j * R + b0 * (R // 2), R // 2), :] + buf0[j]
        flight[j] = send(1, j, acc1.at[j, rows_at((1 - b1) * (R // 4), R // 4)], buf1.at[j], (j + 1) % 4)
    prepare(2)
    prepare(3)
    for j in range(STREAMS):
        b1 = bits[(j + 1) % 4]
        flight[j].wait_recv()
        acc2[j] = acc1[j, rows_at(b1 * (R // 4), R // 4), :] + buf1[j]
        flight[j] = send(2, j, acc2.at[j], buf2.at[j], (j + 2) % 4)
    prepare(4)
    prepare(5)
    for j in range(STREAMS):
        flight[j].wait_recv()
        acc3[j] = acc2[j] + buf2[j]
        flight[j] = send(3, j, acc3.at[j], buf3.at[j], (j + 3) % 4)
    prepare(6)
    prepare(7)
    base = core * OWN
    for j in range(STREAMS):
        b0, b1 = bits[j % 4], bits[(j + 1) % 4]
        here = rows_at(base + j * R + b0 * (R // 2) + b1 * (R // 4), R // 4)
        flight[j].wait_recv()
        land[here, :] = acc3[j] + buf3[j]
        flight[j] = send(4, j, land.at[here], land.at[here], (j + 1) % 4)
    w_send.wait()
    prepare_weights()
    shares = []

    def share(which, start, count):
        here = rows_at(start, count)
        copy = pltpu.make_async_remote_copy(
            land.at[here], land.at[here], sib_send.at[which], sib_recv.at[which],
            device_id=sibling, device_id_type=MESH,
        )
        copy.start()
        shares.append(copy)

    for j in range(STREAMS):
        b0 = bits[j % 4]
        start = base + j * R + b0 * (R // 2)
        flight[j].wait_recv()
        flight[j] = send(5, j, land.at[rows_at(start, R // 2)], land.at[rows_at(start, R // 2)], j % 4)
        share(j, start, R // 2)
    for j in range(STREAMS):
        b0 = bits[j % 4]
        flight[j].wait_recv()
        share(STREAMS + j, base + j * R + (1 - b0) * (R // 2), R // 2)
    for j in range(STREAMS):
        prepare_landmarks(base + j * R, R)
    for copy in shares:
        copy.wait_recv()
    for j in range(STREAMS):
        prepare_landmarks((1 - core) * OWN + j * R, R)

    def ring_copy(t, side):
        return pltpu.make_async_remote_copy(
            sent.at[t, side], got.at[t, side], ring_send.at[t, side], ring_recv.at[t, side],
            device_id=above if side == 0 else below, device_id_type=MESH,
        )

    for t in range(RING):
        inner = lax.dot_general(ll[...], xx[t], (((1,), (1,)), ((), ())), preferred_element_type=F32)
        row = xsq2[t]
        both = lsq2[...]
        logits = inner - jnp.concatenate([both, both], axis=1) - row
        top = jnp.max(logits, axis=0, keepdims=True)
        weight = jnp.exp(logits - top)
        mass = jnp.sum(weight, axis=0, keepdims=True)
        hi, lo = split(weight)
        part = jnp.dot(ww[...], hi, preferred_element_type=F32)
        part = part[:C] + part[C:] + jnp.dot(ww[0:C, :], lo, preferred_element_type=F32)
        for side in range(2):
            lanes = slice(side * HALF, (side + 1) * HALF)
            p, m, s = part[:, lanes], top[:, lanes], mass[:, lanes]
            if t > 0:
                ring_copy(t - 1, side).wait_recv()
                m_in = got[t - 1, side, C : C + 1, :]
                s_in = got[t - 1, side, C + 1 : C + 2, :]
                m_new = jnp.maximum(m, m_in)
                mine, theirs = jnp.exp(m - m_new), jnp.exp(m_in - m_new)
                p = p * mine + got[t - 1, side, 0:C, :] * theirs
                m, s = m_new, s * mine + s_in * theirs
            if t < RING - 1:
                sent[t, side, 0:C, :] = p
                sent[t, side, C : C + 1, :] = m
                sent[t, side, C + 1 : C + 2, :] = s
                sent[t, side, C + 2 :, :] = jnp.zeros((MSG - C - 2, HALF), F32)
                ring_copy(t, side).start()
            else:
                out_ref[side * HALF : (side + 1) * HALF, :] = (p / s).T

    for copy in copies + shares:
        copy.wait_send()
    for t in range(RING - 1):
        for side in range(2):
            ring_copy(t, side).wait_send()


def shards(embeddings, landmark_index, cluster_weights):
    vmem = lambda *shape, dtype=F32: pltpu.VMEM(shape, dtype)
    dma = lambda *shape: pltpu.SemaphoreType.DMA(shape)
    return pl.pallas_call(
        kernel,
        out_shape=jax.ShapeDtypeStruct((CHUNK, C), F32),
        in_specs=[
            pl.BlockSpec(memory_space=pl.ANY),
            pl.BlockSpec(memory_space=pltpu.SMEM),
            pl.BlockSpec(memory_space=pl.ANY),
        ],
        out_specs=pl.BlockSpec(memory_space=pltpu.VMEM),
        scratch_shapes=[
            vmem(ROWS, D),
            vmem(OWN, D),
            vmem(PAIR, D),
            vmem(STREAMS, R // 2, D),
            vmem(STREAMS, R // 4, D),
            vmem(STREAMS, R // 4, D),
            vmem(STREAMS, R // 4, D),
            vmem(STREAMS, R // 2, D),
            vmem(STREAMS, R // 4, D),
            vmem(STREAMS, R // 4, D),
            vmem(PAIR, C),
            vmem(2 * C, PAIR, dtype=BF16),
            vmem(PAIR, 3 * D, dtype=BF16),
            vmem(PAIR, 128),
            vmem(RING, CHUNK, 3 * D, dtype=BF16),
            vmem(RING, 1, CHUNK),
            vmem(RING - 1, 2, MSG, HALF),
            vmem(RING - 1, 2, MSG, HALF),
            dma(LOADS),
            pltpu.SemaphoreType.DMA,
            dma(6, STREAMS),
            dma(6, STREAMS),
            dma(2 * STREAMS),
            dma(2 * STREAMS),
            pltpu.SemaphoreType.DMA,
            pltpu.SemaphoreType.DMA,
            dma(RING - 1, 2),
            dma(RING - 1, 2),
        ],
        compiler_params=pltpu.CompilerParams(
            collective_id=0, has_side_effects=True, vmem_limit_bytes=56 * 2**20
        ),
    )(embeddings, landmark_index, cluster_weights)


def solution(mesh):
    return jax.shard_map(
        shards,
        mesh=mesh,
        in_specs=(P("sample", None), P("landmark"), P("landmark", None)),
        out_specs=P(("sample", "landmark"), None),
        check_vma=False,
    )
```

```python
import jax
import jax.numpy as jnp
from jax import lax
from jax.experimental import pallas as pl
from jax.experimental.pallas import tpu as pltpu
from jax.sharding import PartitionSpec as P

MESH = pl.DeviceIdType.MESH
F32 = jnp.float32
BF16 = jnp.bfloat16

D = 512
C = 256
ROWS = 4096
OWN = 512
PAIR = 2 * OWN
RING = 8
CHUNK = 256
HALF = CHUNK // 2
STREAMS = 8
R = OWN // STREAMS
HEAD = 8
MSG = HEAD + C
SUBS = 4
PART = C // SUBS
BLOCKS = 4
BLOCK = PAIR // BLOCKS
LOADS = 8


def split(a):
    hi = a.astype(BF16)
    return hi, (a - hi.astype(F32)).astype(BF16)


def kernel(
    emb_hbm, idx_ref, w_hbm, out_ref,
    emb, pick, land, buf0, buf1, buf2, buf3, acc1, acc2, acc3,
    wts, ww, ll, lsq2, xx, xsq2, dots0, dots1, held0, held1, sent, got,
    load_sem, w_sem, send_sem, recv_sem, sib_send, sib_recv, ws_send, ws_recv, ring_send, ring_recv,
):
    sample = lax.axis_index("sample")
    mark = lax.axis_index("landmark")
    x, y = sample // 4, sample % 4
    z, core = mark // 2, mark % 2

    partners = [
        ((x + 1 - 2 * (x % 2)) * 4 + y, mark),
        ((3 - x) * 4 + y, mark),
        (x * 4 + y + 1 - 2 * (y % 2), mark),
        (x * 4 + 3 - y, mark),
    ]
    bits = [(x % 2 + x // 2) % 2, x // 2, (y % 2 + y // 2) % 2, y // 2]
    sibling = (sample, z * 2 + 1 - core)
    above = (sample, ((z + 1) % RING) * 2 + core)
    below = (sample, ((z + RING - 1) % RING) * 2 + core)

    barrier = pltpu.get_barrier_semaphore()
    for other in partners + [sibling, above, below]:
        pl.semaphore_signal(barrier, inc=1, device_id=other, device_id_type=MESH)

    loads = []
    for i in range(LOADS):
        part = pl.ds(i * (ROWS // LOADS), ROWS // LOADS)
        load = pltpu.make_async_copy(emb_hbm.at[part], emb.at[part], load_sem.at[i])
        load.start()
        loads.append(load)
    own_w = pl.ds(pl.multiple_of(core * OWN, OWN), OWN)
    w_load = pltpu.make_async_copy(w_hbm, wts.at[own_w], w_sem)
    w_load.start()

    first = sample * ROWS

    def pick_rows(start, count):
        def some(i, carry):
            for u in range(16):
                row = start + i * 16 + u
                place = idx_ref[row] - first
                owned = jnp.logical_and(place >= 0, place < ROWS)
                found = emb[pl.ds(jnp.clip(place, 0, ROWS - 1), 1), :]
                pick[pl.ds(row, 1), :] = jnp.where(owned, found, 0.0)
            return carry

        lax.fori_loop(0, count // 16, some, 0)

    def prepare(t):
        up = ((z + 2 * RING - 1 - t) % RING * 2 + core) * CHUNK
        down = ((z + 1 + t) % RING * 2 + core) * CHUNK + HALF
        for side, start in enumerate((up, down)):
            rows = emb[pl.ds(pl.multiple_of(start, HALF), HALF), :]
            hi, lo = split(4.0 * rows)
            here = pl.ds(side * HALF, HALF)
            xx[t, here, 0:D] = hi
            xx[t, here, D : 2 * D] = lo
            xx[t, here, 2 * D :] = hi
            sq = rows * rows
            sq = (sq[:, 0:128] + sq[:, 128:256]) + (sq[:, 256:384] + sq[:, 384:512])
            xsq2[t, :, side * HALF : (side + 1) * HALF] = 2.0 * jnp.sum(sq.T, axis=0, keepdims=True)

    base = core * OWN
    other_base = (1 - core) * OWN

    def rows_at(start, count):
        return pl.ds(pl.multiple_of(start, 8), count)

    def block_rows(block, j):
        b0 = bits[j % 4]
        late = block // 2
        half = b0 + late - 2 * b0 * late
        return (base if block % 2 == 0 else other_base) + j * R + half * (R // 2)

    def prepare_landmarks(block, j):
        rows = land[rows_at(block_rows(block, j), R // 2), :]
        hi, lo = split(rows)
        here = pl.ds(block * BLOCK + j * (R // 2), R // 2)
        ll[here, 0:D] = hi
        ll[here, D : 2 * D] = hi
        ll[here, 2 * D :] = lo
        lsq2[here, :] = jnp.broadcast_to(2.0 * jnp.sum(rows * rows, axis=1, keepdims=True), (R // 2, 128))

    def prepare_weights(block):
        rows = [wts[rows_at(block_rows(block, j), R // 2), :] for j in range(STREAMS)]
        hi, lo = split(jnp.concatenate(rows, axis=0).T)
        here = slice(block * BLOCK, (block + 1) * BLOCK)
        ww[0:C, here] = hi
        ww[C:, here] = lo

    copies = []

    def send(step, j, src, dst, dim):
        copy = pltpu.make_async_remote_copy(
            src, dst, send_sem.at[step, j], recv_sem.at[step, j],
            device_id=partners[dim], device_id_type=MESH,
        )
        copy.start()
        copies.append(copy)
        return copy

    for load in loads:
        load.wait()
    for j in range(STREAMS):
        pick_rows(j * R + (1 - bits[j % 4]) * (R // 2), R // 2)
    for t in range(RING):
        prepare(t)
    w_load.wait()
    prepare_weights(0)
    prepare_weights(2)

    pl.semaphore_wait(barrier, 7)
    flight = []
    for j in range(STREAMS):
        b0 = bits[j % 4]
        flight.append(send(0, j, pick.at[rows_at(j * R + (1 - b0) * (R // 2), R // 2)], buf0.at[j], j % 4))
    w_send = pltpu.make_async_remote_copy(
        wts.at[own_w], wts.at[own_w], ws_send, ws_recv, device_id=sibling, device_id_type=MESH
    )
    w_send.start()
    for j in range(STREAMS):
        pick_rows(j * R + bits[j % 4] * (R // 2), R // 2)
    for j in range(STREAMS):
        b0, b1 = bits[j % 4], bits[(j + 1) % 4]
        flight[j].wait_recv()
        acc1[j] = pick[rows_at(j * R + b0 * (R // 2), R // 2), :] + buf0[j]
        flight[j] = send(1, j, acc1.at[j, rows_at((1 - b1) * (R // 4), R // 4)], buf1.at[j], (j + 1) % 4)
    for j in range(STREAMS):
        b1 = bits[(j + 1) % 4]
        flight[j].wait_recv()
        acc2[j] = acc1[j, rows_at(b1 * (R // 4), R // 4), :] + buf1[j]
        flight[j] = send(2, j, acc2.at[j], buf2.at[j], (j + 2) % 4)
    w_send.wait()
    prepare_weights(1)
    for j in range(STREAMS):
        flight[j].wait_recv()
        acc3[j] = acc2[j] + buf2[j]
        flight[j] = send(3, j, acc3.at[j], buf3.at[j], (j + 3) % 4)
    prepare_weights(3)
    for j in range(STREAMS):
        b0, b1 = bits[j % 4], bits[(j + 1) % 4]
        here = rows_at(base + j * R + b0 * (R // 2) + b1 * (R // 4), R // 4)
        flight[j].wait_recv()
        land[here, :] = acc3[j] + buf3[j]
        flight[j] = send(4, j, land.at[here], land.at[here], (j + 1) % 4)
    shares = []

    def share(which, start, count):
        here = rows_at(start, count)
        copy = pltpu.make_async_remote_copy(
            land.at[here], land.at[here], sib_send.at[which], sib_recv.at[which],
            device_id=sibling, device_id_type=MESH,
        )
        copy.start()
        shares.append(copy)

    for j in range(STREAMS):
        here = rows_at(block_rows(0, j), R // 2)
        flight[j].wait_recv()
        flight[j] = send(5, j, land.at[here], land.at[here], j % 4)
        share(j, block_rows(0, j), R // 2)
    for j in range(STREAMS):
        prepare_landmarks(0, j)

    dots = (dots0, dots1)
    held = (held0, held1)
    tops = [None] * RING

    def inner(t, block):
        here = slice(block * BLOCK, (block + 1) * BLOCK)
        product = lax.dot_general(ll[here, :], xx[t], (((1,), (1,)), ((), ())), preferred_element_type=F32)
        both = lsq2[here, :]
        logits = product - jnp.concatenate([both, both], axis=1) - xsq2[t]
        dots[t % 2][here, :] = logits
        top = jnp.max(logits, axis=0, keepdims=True)
        tops[t] = top if tops[t] is None else jnp.maximum(tops[t], top)

    def outer(t, block, total, mass):
        here = slice(block * BLOCK, (block + 1) * BLOCK)
        weight = jnp.exp(dots[t % 2][here, :] - tops[t])
        hi, lo = split(weight)
        part = jnp.dot(ww[:, here], hi, preferred_element_type=F32)
        part = part[:C] + part[C:] + jnp.dot(ww[0:C, here], lo, preferred_element_type=F32)
        here_mass = jnp.sum(weight, axis=0, keepdims=True)
        if total is None:
            return part, here_mass
        return total + part, mass + here_mass

    def piece_rows(piece):
        return slice(0 if piece == 0 else HEAD + piece * PART, HEAD + (piece + 1) * PART)

    def ring_copy(t, side, piece):
        here = piece_rows(piece)
        here = pl.ds(here.start, here.stop - here.start)
        return pltpu.make_async_remote_copy(
            sent.at[t, side, here], got.at[t, side, here], ring_send.at[t, side, piece], ring_recv.at[t, side, piece],
            device_id=above if side == 0 else below, device_id_type=MESH,
        )

    scales = {}

    def handle(t, piece):
        mine_ref = held[t % 2]
        for side in range(2):
            lanes = slice(side * HALF, (side + 1) * HALF)
            if t > 0:
                ring_copy(t - 1, side, piece).wait_recv()
            if piece == 0:
                m, s = mine_ref[0:1, lanes], mine_ref[1:2, lanes]
                mine = theirs = None
                if t > 0:
                    m_in, s_in = got[t - 1, side, 0:1, :], got[t - 1, side, 1:2, :]
                    m_new = jnp.maximum(m, m_in)
                    mine, theirs = jnp.exp(m - m_new), jnp.exp(m_in - m_new)
                    m, s = m_new, s * mine + s_in * theirs
                if t < RING - 1:
                    sent[t, side, 0:HEAD, :] = jnp.concatenate([m, s, jnp.zeros((HEAD - 2, HALF), F32)], axis=0)
                scales[side] = mine, theirs, s
            mine, theirs, s = scales[side]
            rows = slice(HEAD + piece * PART, HEAD + (piece + 1) * PART)
            p = mine_ref[rows, lanes]
            if t > 0:
                p = p * mine + got[t - 1, side, rows, :] * theirs
            if t < RING - 1:
                sent[t, side, rows, :] = p
                ring_copy(t, side, piece).start()
            else:
                mine_ref[rows, lanes] = p / s

    for j in range(STREAMS):
        shares[j].wait_recv()
        prepare_landmarks(1, j)
    for t in range(2):
        for block in range(2):
            inner(t, block)
    for j in range(STREAMS):
        flight[j].wait_recv()
        share(STREAMS + j, block_rows(2, j), R // 2)
    for j in range(STREAMS):
        prepare_landmarks(2, j)
    inner(0, 2)
    for j in range(STREAMS):
        shares[STREAMS + j].wait_recv()
        prepare_landmarks(3, j)
    inner(0, 3)

    for t in range(RING):
        total = mass = None
        for block in range(BLOCKS):
            if t + 1 < RING and not (t == 0 and block < 2):
                inner(t + 1, block)
            total, mass = outer(t, block, total, mass)
            if t >= 2 and block < SUBS:
                handle(t - 1, block)
        held[t % 2][0:1, :] = tops[t]
        held[t % 2][1:2, :] = mass
        held[t % 2][HEAD:, :] = total
        if t == 0:
            for piece in range(SUBS):
                handle(0, piece)
    last = RING - 1
    for piece in range(SUBS):
        handle(last, piece)
        if (piece + 1) * PART % 128 == 0:
            done = (piece + 1) * PART
            out_ref[:, done - 128 : done] = held[last % 2][HEAD + done - 128 : HEAD + done, :].T

    for copy in copies + shares:
        copy.wait_send()
    for t in range(RING - 1):
        for side in range(2):
            for piece in range(SUBS):
                ring_copy(t, side, piece).wait_send()


def shards(embeddings, landmark_index, cluster_weights):
    vmem = lambda *shape, dtype=F32: pltpu.VMEM(shape, dtype)
    dma = lambda *shape: pltpu.SemaphoreType.DMA(shape)
    return pl.pallas_call(
        kernel,
        out_shape=jax.ShapeDtypeStruct((CHUNK, C), F32),
        in_specs=[
            pl.BlockSpec(memory_space=pl.ANY),
            pl.BlockSpec(memory_space=pltpu.SMEM),
            pl.BlockSpec(memory_space=pl.ANY),
        ],
        out_specs=pl.BlockSpec(memory_space=pltpu.VMEM),
        scratch_shapes=[
            vmem(ROWS, D),
            vmem(OWN, D),
            vmem(PAIR, D),
            vmem(STREAMS, R // 2, D),
            vmem(STREAMS, R // 4, D),
            vmem(STREAMS, R // 4, D),
            vmem(STREAMS, R // 4, D),
            vmem(STREAMS, R // 2, D),
            vmem(STREAMS, R // 4, D),
            vmem(STREAMS, R // 4, D),
            vmem(PAIR, C),
            vmem(2 * C, PAIR, dtype=BF16),
            vmem(PAIR, 3 * D, dtype=BF16),
            vmem(PAIR, 128),
            vmem(RING, CHUNK, 3 * D, dtype=BF16),
            vmem(RING, 1, CHUNK),
            vmem(PAIR, CHUNK),
            vmem(PAIR, CHUNK),
            vmem(MSG, CHUNK),
            vmem(MSG, CHUNK),
            vmem(RING - 1, 2, MSG, HALF),
            vmem(RING - 1, 2, MSG, HALF),
            dma(LOADS),
            pltpu.SemaphoreType.DMA,
            dma(6, STREAMS),
            dma(6, STREAMS),
            dma(2 * STREAMS),
            dma(2 * STREAMS),
            pltpu.SemaphoreType.DMA,
            pltpu.SemaphoreType.DMA,
            dma(RING - 1, 2, SUBS),
            dma(RING - 1, 2, SUBS),
        ],
        compiler_params=pltpu.CompilerParams(
            collective_id=0, has_side_effects=True, vmem_limit_bytes=56 * 2**20
        ),
    )(embeddings, landmark_index, cluster_weights)


def solution(mesh):
    return jax.shard_map(
        shards,
        mesh=mesh,
        in_specs=(P("sample", None), P("landmark"), P("landmark", None)),
        out_specs=P(("sample", "landmark"), None),
        check_vma=False,
    )
```

```python
import jax
import jax.numpy as jnp
from jax import lax
from jax.experimental import pallas as pl
from jax.experimental.pallas import tpu as pltpu
from jax.sharding import PartitionSpec as P

MESH = pl.DeviceIdType.MESH
F32 = jnp.float32
BF16 = jnp.bfloat16

D = 512
C = 256
ROWS = 4096
OWN = 512
PAIR = 2 * OWN
RING = 8
CHUNK = 256
HALF = CHUNK // 2
STREAMS = 8
R = OWN // STREAMS
HEAD = 8
MSG = HEAD + C
SUBS = 2
PART = C // SUBS
BLOCKS = 4
BLOCK = PAIR // BLOCKS
LOADS = 8
ORDER = (4, 3, -3, 2, -2, 1, -1, 0)
UNITS = RING - 1


def split(a):
    hi = a.astype(BF16)
    return hi, (a - hi.astype(F32)).astype(BF16)


def kernel(
    emb_hbm, idx_ref, w_hbm, out_ref,
    emb, pick, land, buf0, buf1, buf2, buf3, acc1, acc2, acc3,
    wts, ww, ll, lsq2, xx, xsq2, dots0, dots1, held, sent, got,
    load_sem, w_sem, send_sem, recv_sem, sib_send, sib_recv, ws_send, ws_recv, ring_send, ring_recv,
):
    sample = lax.axis_index("sample")
    mark = lax.axis_index("landmark")
    x, y = sample // 4, sample % 4
    z, core = mark // 2, mark % 2

    partners = [
        ((x + 1 - 2 * (x % 2)) * 4 + y, mark),
        ((3 - x) * 4 + y, mark),
        (x * 4 + y + 1 - 2 * (y % 2), mark),
        (x * 4 + 3 - y, mark),
    ]
    bits = [(x % 2 + x // 2) % 2, x // 2, (y % 2 + y // 2) % 2, y // 2]
    sibling = (sample, z * 2 + 1 - core)
    above = (sample, ((z + 1) % RING) * 2 + core)
    below = (sample, ((z + RING - 1) % RING) * 2 + core)

    barrier = pltpu.get_barrier_semaphore()
    for other in partners + [sibling, above, below]:
        pl.semaphore_signal(barrier, inc=1, device_id=other, device_id_type=MESH)

    loads = []
    for i in range(LOADS):
        part = pl.ds(i * (ROWS // LOADS), ROWS // LOADS)
        load = pltpu.make_async_copy(emb_hbm.at[part], emb.at[part], load_sem.at[i])
        load.start()
        loads.append(load)
    own_w = pl.ds(pl.multiple_of(core * OWN, OWN), OWN)
    w_load = pltpu.make_async_copy(w_hbm, wts.at[own_w], w_sem)
    w_load.start()

    first = sample * ROWS

    def pick_rows(start, count):
        def some(i, carry):
            for u in range(16):
                row = start + i * 16 + u
                place = idx_ref[row] - first
                owned = jnp.logical_and(place >= 0, place < ROWS)
                found = emb[pl.ds(jnp.clip(place, 0, ROWS - 1), 1), :]
                pick[pl.ds(row, 1), :] = jnp.where(owned, found, 0.0)
            return carry

        lax.fori_loop(0, count // 16, some, 0)

    def prepare(t):
        chip = (z + RING + ORDER[t]) % RING
        rows = emb[pl.ds(pl.multiple_of((chip * 2 + core) * CHUNK, CHUNK), CHUNK), :]
        hi, lo = split(4.0 * rows)
        xx[t, :, 0:D] = hi
        xx[t, :, D : 2 * D] = lo
        xx[t, :, 2 * D :] = hi
        sq = rows * rows
        sq = (sq[:, 0:128] + sq[:, 128:256]) + (sq[:, 256:384] + sq[:, 384:512])
        xsq2[t] = 2.0 * jnp.sum(sq.T, axis=0, keepdims=True)

    base = core * OWN
    other_base = (1 - core) * OWN

    def rows_at(start, count):
        return pl.ds(pl.multiple_of(start, 8), count)

    def block_rows(block, j):
        b0 = bits[j % 4]
        late = block // 2
        half = b0 + late - 2 * b0 * late
        return (base if block % 2 == 0 else other_base) + j * R + half * (R // 2)

    def prepare_landmarks(block, j):
        rows = land[rows_at(block_rows(block, j), R // 2), :]
        hi, lo = split(rows)
        here = pl.ds(block * BLOCK + j * (R // 2), R // 2)
        ll[here, 0:D] = hi
        ll[here, D : 2 * D] = hi
        ll[here, 2 * D :] = lo
        lsq2[here, :] = jnp.broadcast_to(2.0 * jnp.sum(rows * rows, axis=1, keepdims=True), (R // 2, 128))

    def prepare_weights(block):
        rows = [wts[rows_at(block_rows(block, j), R // 2), :] for j in range(STREAMS)]
        hi, lo = split(jnp.concatenate(rows, axis=0).T)
        here = slice(block * BLOCK, (block + 1) * BLOCK)
        ww[0:C, here] = hi
        ww[C:, here] = lo

    copies = []

    def send(step, j, src, dst, dim):
        copy = pltpu.make_async_remote_copy(
            src, dst, send_sem.at[step, j], recv_sem.at[step, j],
            device_id=partners[dim], device_id_type=MESH,
        )
        copy.start()
        copies.append(copy)
        return copy

    groups = [range(g, g + 4) for g in range(0, STREAMS, 4)]
    flight = [None] * STREAMS
    shares = [None] * (2 * STREAMS)

    def pick_half(j, half):
        pick_rows(j * R + half * (R // 2), R // 2)

    def halve_first(j):
        b0 = bits[j % 4]
        flight[j] = send(0, j, pick.at[rows_at(j * R + (1 - b0) * (R // 2), R // 2)], buf0.at[j], j % 4)

    def halve_second(j):
        b0, b1 = bits[j % 4], bits[(j + 1) % 4]
        flight[j].wait_recv()
        acc1[j] = pick[rows_at(j * R + b0 * (R // 2), R // 2), :] + buf0[j]
        flight[j] = send(1, j, acc1.at[j, rows_at((1 - b1) * (R // 4), R // 4)], buf1.at[j], (j + 1) % 4)

    def exchange_first(j):
        b1 = bits[(j + 1) % 4]
        flight[j].wait_recv()
        acc2[j] = acc1[j, rows_at(b1 * (R // 4), R // 4), :] + buf1[j]
        flight[j] = send(2, j, acc2.at[j], buf2.at[j], (j + 2) % 4)

    def exchange_second(j):
        flight[j].wait_recv()
        acc3[j] = acc2[j] + buf2[j]
        flight[j] = send(3, j, acc3.at[j], buf3.at[j], (j + 3) % 4)

    def gather_first(j):
        b0, b1 = bits[j % 4], bits[(j + 1) % 4]
        here = rows_at(base + j * R + b0 * (R // 2) + b1 * (R // 4), R // 4)
        flight[j].wait_recv()
        land[here, :] = acc3[j] + buf3[j]
        flight[j] = send(4, j, land.at[here], land.at[here], (j + 1) % 4)

    def share(which, start, count):
        here = rows_at(start, count)
        copy = pltpu.make_async_remote_copy(
            land.at[here], land.at[here], sib_send.at[which], sib_recv.at[which],
            device_id=sibling, device_id_type=MESH,
        )
        copy.start()
        shares[which] = copy

    def gather_second(j):
        here = rows_at(block_rows(0, j), R // 2)
        flight[j].wait_recv()
        flight[j] = send(5, j, land.at[here], land.at[here], j % 4)
        share(j, block_rows(0, j), R // 2)

    def finish(j):
        flight[j].wait_recv()
        share(STREAMS + j, block_rows(2, j), R // 2)

    for load in loads:
        load.wait()
    for g, group in enumerate(groups):
        for j in group:
            pick_half(j, 1 - bits[j % 4])
        if g == 0:
            pl.semaphore_wait(barrier, 7)
        for j in group:
            halve_first(j)
        if g == 0:
            prepare(0)
            prepare(1)
    w_load.wait()
    w_send = pltpu.make_async_remote_copy(
        wts.at[own_w], wts.at[own_w], ws_send, ws_recv, device_id=sibling, device_id_type=MESH
    )
    w_send.start()
    for j in range(STREAMS):
        pick_half(j, bits[j % 4])
    fillers = [
        lambda: (prepare(2), prepare(3), prepare(4), prepare(5)),
        lambda: (prepare(6), prepare(7)),
        lambda: (prepare_weights(0), prepare_weights(2)),
        lambda: (w_send.wait_recv(), prepare_weights(1), prepare_weights(3)),
    ]
    for stage in (halve_second, exchange_first, exchange_second, gather_first, gather_second):
        for group in groups:
            for j in group:
                stage(j)
            if fillers:
                fillers.pop(0)()
    for j in range(STREAMS):
        prepare_landmarks(0, j)

    dots = (dots0, dots1)
    tops = [None] * RING

    def inner(t, block):
        here = slice(block * BLOCK, (block + 1) * BLOCK)
        product = lax.dot_general(ll[here, :], xx[t], (((1,), (1,)), ((), ())), preferred_element_type=F32)
        both = lsq2[here, :]
        logits = product - jnp.concatenate([both, both], axis=1) - xsq2[t]
        dots[t % 2][here, :] = logits
        top = jnp.max(logits, axis=0, keepdims=True)
        tops[t] = top if tops[t] is None else jnp.maximum(tops[t], top)

    def outer(t, block, total, mass):
        here = slice(block * BLOCK, (block + 1) * BLOCK)
        weight = jnp.exp(dots[t % 2][here, :] - tops[t])
        hi, lo = split(weight)
        part = jnp.dot(ww[:, here], hi, preferred_element_type=F32)
        part = part[:C] + part[C:] + jnp.dot(ww[0:C, here], lo, preferred_element_type=F32)
        here_mass = jnp.sum(weight, axis=0, keepdims=True)
        if total is None:
            return part, here_mass
        return total + part, mass + here_mass

    def piece_rows(piece):
        return slice(0 if piece == 0 else HEAD + piece * PART, HEAD + (piece + 1) * PART)

    def ring_copy(unit, side, piece):
        here = piece_rows(piece)
        here = pl.ds(here.start, here.stop - here.start)
        return pltpu.make_async_remote_copy(
            sent.at[unit, side, here], got.at[unit, side, here],
            ring_send.at[unit, side, piece], ring_recv.at[unit, side, piece],
            device_id=above if side == 0 else below, device_id_type=MESH,
        )

    def lanes_of(half):
        return slice(half * HALF, (half + 1) * HALF)

    scales = {}

    def merge(key, piece, chunk, half, incoming):
        if piece == 0:
            m, s = held[chunk, 0:1, lanes_of(half)], held[chunk, 1:2, lanes_of(half)]
            factors = []
            if incoming:
                m_in = [got[u, side, 0:1, :] for u, side in incoming]
                top = m
                for other in m_in:
                    top = jnp.maximum(top, other)
                factors = [jnp.exp(other - top) for other in [m] + m_in]
                s = s * factors[0]
                for (u, side), factor in zip(incoming, factors[1:]):
                    s = s + got[u, side, 1:2, :] * factor
                m = top
            scales[key] = factors, m, s
        factors = scales[key][0]
        rows = slice(HEAD + piece * PART, HEAD + (piece + 1) * PART)
        p = held[chunk, rows, lanes_of(half)]
        if incoming:
            p = p * factors[0]
            for (u, side), factor in zip(incoming, factors[1:]):
                p = p + got[u, side, rows, :] * factor
        return p

    def handle(unit, sides=(0, 1)):
        hop = (unit + 1) // 2
        for piece in range(SUBS):
            for side in sides:
                incoming = []
                if unit >= 2:
                    ring_copy(unit - 2, side, piece).wait_recv()
                    incoming = [(unit - 2, side)]
                chunk = 0 if hop == 0 else 2 * hop - 1 + side
                half = (unit + side) % 2
                p = merge((unit, side), piece, chunk, half, incoming)
                if piece == 0:
                    m, s = scales[unit, side][1:]
                    sent[unit, side, 0:HEAD, :] = jnp.concatenate([m, s, jnp.zeros((HEAD - 2, HALF), F32)], axis=0)
                sent[unit, side, HEAD + piece * PART : HEAD + (piece + 1) * PART, :] = p
                ring_copy(unit, side, piece).start()

    for j in range(STREAMS):
        shares[j].wait_recv()
        prepare_landmarks(1, j)
    for t in range(2):
        for block in range(2):
            inner(t, block)
    for group in groups:
        for j in group:
            finish(j)
        for j in group:
            prepare_landmarks(2, j)
    inner(0, 2)
    for j in range(STREAMS):
        shares[STREAMS + j].wait_recv()
        prepare_landmarks(3, j)
    inner(0, 3)

    for t in range(RING):
        total = mass = None
        for block in range(BLOCKS):
            if t + 1 < RING and not (t == 0 and block < 2):
                inner(t + 1, block)
            total, mass = outer(t, block, total, mass)
        held[t, 0:1, :] = tops[t]
        held[t, 1:2, :] = mass
        held[t, HEAD:, :] = total
        if t == 0:
            handle(0)
        elif t == 1:
            handle(1, (0,))
        elif t == 2:
            handle(1, (1,))
        elif t == 4:
            handle(2)
        elif t == 6:
            handle(3)
    for unit in range(4, UNITS):
        handle(unit)
    for piece in range(SUBS):
        for unit in (UNITS - 2, UNITS - 1):
            for side in range(2):
                ring_copy(unit, side, piece).wait_recv()
        for half in range(2):
            incoming = [(UNITS - 1 - half, 0), (UNITS - 2 + half, 1)]
            p = merge(half, piece, RING - 1, half, incoming) / scales[half][2]
            out_ref[lanes_of(half), piece * PART : (piece + 1) * PART] = p.T

    w_send.wait_send()
    for copy in copies + shares:
        copy.wait_send()
    for unit in range(UNITS):
        for side in range(2):
            for piece in range(SUBS):
                ring_copy(unit, side, piece).wait_send()


def shards(embeddings, landmark_index, cluster_weights):
    vmem = lambda *shape, dtype=F32: pltpu.VMEM(shape, dtype)
    dma = lambda *shape: pltpu.SemaphoreType.DMA(shape)
    return pl.pallas_call(
        kernel,
        out_shape=jax.ShapeDtypeStruct((CHUNK, C), F32),
        in_specs=[
            pl.BlockSpec(memory_space=pl.ANY),
            pl.BlockSpec(memory_space=pltpu.SMEM),
            pl.BlockSpec(memory_space=pl.ANY),
        ],
        out_specs=pl.BlockSpec(memory_space=pltpu.VMEM),
        scratch_shapes=[
            vmem(ROWS, D),
            vmem(OWN, D),
            vmem(PAIR, D),
            vmem(STREAMS, R // 2, D),
            vmem(STREAMS, R // 4, D),
            vmem(STREAMS, R // 4, D),
            vmem(STREAMS, R // 4, D),
            vmem(STREAMS, R // 2, D),
            vmem(STREAMS, R // 4, D),
            vmem(STREAMS, R // 4, D),
            vmem(PAIR, C),
            vmem(2 * C, PAIR, dtype=BF16),
            vmem(PAIR, 3 * D, dtype=BF16),
            vmem(PAIR, 128),
            vmem(RING, CHUNK, 3 * D, dtype=BF16),
            vmem(RING, 1, CHUNK),
            vmem(PAIR, CHUNK),
            vmem(PAIR, CHUNK),
            vmem(RING, MSG, CHUNK),
            vmem(UNITS, 2, MSG, HALF),
            vmem(UNITS, 2, MSG, HALF),
            dma(LOADS),
            pltpu.SemaphoreType.DMA,
            dma(6, STREAMS),
            dma(6, STREAMS),
            dma(2 * STREAMS),
            dma(2 * STREAMS),
            pltpu.SemaphoreType.DMA,
            pltpu.SemaphoreType.DMA,
            dma(UNITS, 2, SUBS),
            dma(UNITS, 2, SUBS),
        ],
        compiler_params=pltpu.CompilerParams(
            collective_id=0, has_side_effects=True, vmem_limit_bytes=56 * 2**20
        ),
    )(embeddings, landmark_index, cluster_weights)


def solution(mesh):
    return jax.shard_map(
        shards,
        mesh=mesh,
        in_specs=(P("sample", None), P("landmark"), P("landmark", None)),
        out_specs=P(("sample", "landmark"), None),
        check_vma=False,
    )
```

```python
import jax
import jax.numpy as jnp
from jax import lax
from jax.experimental import pallas as pl
from jax.experimental.pallas import tpu as pltpu
from jax.sharding import PartitionSpec as P

MESH = pl.DeviceIdType.MESH
F32 = jnp.float32
BF16 = jnp.bfloat16

D = 512
C = 256
ROWS = 4096
OWN = 512
PAIR = 2 * OWN
RING = 8
CHUNK = 256
HALF = CHUNK // 2
STREAMS = 8
R = OWN // STREAMS
HEAD = 8
MSG = HEAD + C
SUBS = 2
PART = C // SUBS
BLOCKS = 4
BLOCK = PAIR // BLOCKS
LOADS = 8
ORDER = (4, 3, -3, 2, -2, 1, -1, 0)
UNITS = RING - 1


def split(a):
    hi = a.astype(BF16)
    return hi, (a - hi.astype(F32)).astype(BF16)


def kernel(
    emb_hbm, idx_ref, w_hbm, out_ref,
    emb, pick, land, buf0, buf1, buf2, buf3, acc1, acc2, acc3,
    wts, ww, ll, lsq2, xx, xsq2, dots0, dots1, held, sent, got,
    load_sem, w_sem, send_sem, recv_sem, sib_send, sib_recv, ws_send, ws_recv, ring_send, ring_recv,
):
    sample = lax.axis_index("sample")
    mark = lax.axis_index("landmark")
    x, y = sample // 4, sample % 4
    z, core = mark // 2, mark % 2

    partners = [
        ((x + 1 - 2 * (x % 2)) * 4 + y, mark),
        ((3 - x) * 4 + y, mark),
        (x * 4 + y + 1 - 2 * (y % 2), mark),
        (x * 4 + 3 - y, mark),
    ]
    bits = [(x % 2 + x // 2) % 2, x // 2, (y % 2 + y // 2) % 2, y // 2]
    sibling = (sample, z * 2 + 1 - core)
    above = (sample, ((z + 1) % RING) * 2 + core)
    below = (sample, ((z + RING - 1) % RING) * 2 + core)

    loads = []
    for i in range(LOADS):
        part = pl.ds(i * (ROWS // LOADS), ROWS // LOADS)
        load = pltpu.make_async_copy(emb_hbm.at[part], emb.at[part], load_sem.at[i])
        load.start()
        loads.append(load)
    own_w = pl.ds(pl.multiple_of(core * OWN, OWN), OWN)
    w_load = pltpu.make_async_copy(w_hbm, wts.at[own_w], w_sem)
    w_load.start()

    barrier = pltpu.get_barrier_semaphore()
    for other in partners + [sibling, above, below]:
        pl.semaphore_signal(barrier, inc=1, device_id=other, device_id_type=MESH)

    first = sample * ROWS

    def pick_rows(start, count):
        def some(i, carry):
            for u in range(16):
                row = start + i * 16 + u
                place = idx_ref[row] - first
                owned = jnp.logical_and(place >= 0, place < ROWS)
                found = emb[pl.ds(jnp.clip(place, 0, ROWS - 1), 1), :]
                pick[pl.ds(row, 1), :] = jnp.where(owned, found, 0.0)
            return carry

        lax.fori_loop(0, count // 16, some, 0)

    def prepare(t):
        chip = (z + RING + ORDER[t]) % RING
        rows = emb[pl.ds(pl.multiple_of((chip * 2 + core) * CHUNK, CHUNK), CHUNK), :]
        hi, lo = split(4.0 * rows)
        xx[t, :, 0:D] = hi
        xx[t, :, D : 2 * D] = lo
        xx[t, :, 2 * D :] = hi
        sq = rows * rows
        sq = (sq[:, 0:128] + sq[:, 128:256]) + (sq[:, 256:384] + sq[:, 384:512])
        xsq2[t] = 2.0 * jnp.sum(sq.T, axis=0, keepdims=True)

    base = core * OWN
    other_base = (1 - core) * OWN

    def rows_at(start, count):
        return pl.ds(pl.multiple_of(start, 8), count)

    def block_rows(block, j):
        b0 = bits[j % 4]
        late = block // 2
        half = b0 + late - 2 * b0 * late
        return (base if block % 2 == 0 else other_base) + j * R + half * (R // 2)

    def prepare_landmarks(block, j):
        rows = land[rows_at(block_rows(block, j), R // 2), :]
        hi, lo = split(rows)
        here = pl.ds(block * BLOCK + j * (R // 2), R // 2)
        ll[here, 0:D] = hi
        ll[here, D : 2 * D] = hi
        ll[here, 2 * D :] = lo
        lsq2[here, :] = jnp.broadcast_to(2.0 * jnp.sum(rows * rows, axis=1, keepdims=True), (R // 2, 128))

    def prepare_weights(block):
        rows = [wts[rows_at(block_rows(block, j), R // 2), :] for j in range(STREAMS)]
        hi, lo = split(jnp.concatenate(rows, axis=0).T)
        here = slice(block * BLOCK, (block + 1) * BLOCK)
        ww[0:C, here] = hi
        ww[C:, here] = lo

    copies = []

    def send(step, j, src, dst, dim):
        copy = pltpu.make_async_remote_copy(
            src, dst, send_sem.at[step, j], recv_sem.at[step, j],
            device_id=partners[dim], device_id_type=MESH,
        )
        copy.start()
        copies.append(copy)
        return copy

    groups = [range(g, g + 4) for g in range(0, STREAMS, 4)]
    flight = [None] * STREAMS
    shares = [None] * (2 * STREAMS)

    def pick_half(j, half):
        pick_rows(j * R + half * (R // 2), R // 2)

    def halve_first(j):
        b0 = bits[j % 4]
        flight[j] = send(0, j, pick.at[rows_at(j * R + (1 - b0) * (R // 2), R // 2)], buf0.at[j], j % 4)

    def halve_second(j):
        b0, b1 = bits[j % 4], bits[(j + 1) % 4]
        flight[j].wait_recv()
        acc1[j] = pick[rows_at(j * R + b0 * (R // 2), R // 2), :] + buf0[j]
        flight[j] = send(1, j, acc1.at[j, rows_at((1 - b1) * (R // 4), R // 4)], buf1.at[j], (j + 1) % 4)

    def exchange_first(j):
        b1 = bits[(j + 1) % 4]
        flight[j].wait_recv()
        acc2[j] = acc1[j, rows_at(b1 * (R // 4), R // 4), :] + buf1[j]
        flight[j] = send(2, j, acc2.at[j], buf2.at[j], (j + 2) % 4)

    def exchange_second(j):
        flight[j].wait_recv()
        acc3[j] = acc2[j] + buf2[j]
        flight[j] = send(3, j, acc3.at[j], buf3.at[j], (j + 3) % 4)

    def gather_first(j):
        b0, b1 = bits[j % 4], bits[(j + 1) % 4]
        here = rows_at(base + j * R + b0 * (R // 2) + b1 * (R // 4), R // 4)
        flight[j].wait_recv()
        land[here, :] = acc3[j] + buf3[j]
        flight[j] = send(4, j, land.at[here], land.at[here], (j + 1) % 4)

    def share(which, start, count):
        here = rows_at(start, count)
        copy = pltpu.make_async_remote_copy(
            land.at[here], land.at[here], sib_send.at[which], sib_recv.at[which],
            device_id=sibling, device_id_type=MESH,
        )
        copy.start()
        shares[which] = copy

    def gather_second(j):
        here = rows_at(block_rows(0, j), R // 2)
        flight[j].wait_recv()
        flight[j] = send(5, j, land.at[here], land.at[here], j % 4)
        share(j, block_rows(0, j), R // 2)

    def finish(j):
        flight[j].wait_recv()
        share(STREAMS + j, block_rows(2, j), R // 2)

    for load in loads:
        load.wait()
    for g, group in enumerate(groups):
        for j in group:
            pick_half(j, 1 - bits[j % 4])
        if g == 0:
            pl.semaphore_wait(barrier, 7)
        for j in group:
            halve_first(j)
        if g == 0:
            prepare(0)
            prepare(1)
    w_load.wait()
    w_send = pltpu.make_async_remote_copy(
        wts.at[own_w], wts.at[own_w], ws_send, ws_recv, device_id=sibling, device_id_type=MESH
    )
    w_send.start()
    for j in range(STREAMS):
        pick_half(j, bits[j % 4])
    fillers = [
        lambda: (prepare(2), prepare(3), prepare(4), prepare(5)),
        lambda: (prepare(6), prepare(7)),
        lambda: (prepare_weights(0), prepare_weights(2)),
        lambda: (w_send.wait_recv(), prepare_weights(1), prepare_weights(3)),
    ]
    for stage in (halve_second, exchange_first, exchange_second, gather_first, gather_second):
        for group in groups:
            for j in group:
                stage(j)
            if fillers:
                fillers.pop(0)()
    for j in range(STREAMS):
        prepare_landmarks(0, j)

    dots = (dots0, dots1)
    tops = [None] * RING

    def inner(t, block):
        here = slice(block * BLOCK, (block + 1) * BLOCK)
        product = lax.dot_general(ll[here, :], xx[t], (((1,), (1,)), ((), ())), preferred_element_type=F32)
        both = lsq2[here, :]
        logits = product - jnp.concatenate([both, both], axis=1) - xsq2[t]
        dots[t % 2][here, :] = logits
        top = jnp.max(logits, axis=0, keepdims=True)
        tops[t] = top if tops[t] is None else jnp.maximum(tops[t], top)

    def outer(t, block, total, mass, top):
        here = slice(block * BLOCK, (block + 1) * BLOCK)
        weight = jnp.exp(dots[t % 2][here, :] - top)
        hi, lo = split(weight)
        part = jnp.dot(ww[:, here], hi, preferred_element_type=F32)
        part = part[:C] + part[C:] + jnp.dot(ww[0:C, here], lo, preferred_element_type=F32)
        here_mass = jnp.sum(weight, axis=0, keepdims=True)
        if total is None:
            return part, here_mass
        return total + part, mass + here_mass

    def first_chunk(block, old):
        inner(0, block)
        if block == 0:
            total, mass = outer(0, 0, None, None, tops[0])
        else:
            shrink = jnp.exp(old - tops[0])
            total, mass = outer(0, block, held[0, HEAD:, :] * shrink, held[0, 1:2, :] * shrink, tops[0])
        held[0, 0:1, :] = tops[0]
        held[0, 1:2, :] = mass
        held[0, HEAD:, :] = total
        return tops[0]

    def piece_rows(piece):
        return slice(0 if piece == 0 else HEAD + piece * PART, HEAD + (piece + 1) * PART)

    def ring_copy(unit, side, piece):
        here = piece_rows(piece)
        here = pl.ds(here.start, here.stop - here.start)
        return pltpu.make_async_remote_copy(
            sent.at[unit, side, here], got.at[unit, side, here],
            ring_send.at[unit, side, piece], ring_recv.at[unit, side, piece],
            device_id=above if side == 0 else below, device_id_type=MESH,
        )

    def lanes_of(half):
        return slice(half * HALF, (half + 1) * HALF)

    scales = {}

    def merge(key, piece, chunk, half, incoming):
        if piece == 0:
            m, s = held[chunk, 0:1, lanes_of(half)], held[chunk, 1:2, lanes_of(half)]
            factors = []
            if incoming:
                m_in = [got[u, side, 0:1, :] for u, side in incoming]
                top = m
                for other in m_in:
                    top = jnp.maximum(top, other)
                factors = [jnp.exp(other - top) for other in [m] + m_in]
                s = s * factors[0]
                for (u, side), factor in zip(incoming, factors[1:]):
                    s = s + got[u, side, 1:2, :] * factor
                m = top
            scales[key] = factors, m, s
        factors = scales[key][0]
        rows = slice(HEAD + piece * PART, HEAD + (piece + 1) * PART)
        p = held[chunk, rows, lanes_of(half)]
        if incoming:
            p = p * factors[0]
            for (u, side), factor in zip(incoming, factors[1:]):
                p = p + got[u, side, rows, :] * factor
        return p

    def handle(unit, sides=(0, 1)):
        hop = (unit + 1) // 2
        for piece in range(SUBS):
            for side in sides:
                incoming = []
                if unit >= 2:
                    ring_copy(unit - 2, side, piece).wait_recv()
                    incoming = [(unit - 2, side)]
                chunk = 0 if hop == 0 else 2 * hop - 1 + side
                half = (unit + side) % 2
                p = merge((unit, side), piece, chunk, half, incoming)
                if piece == 0:
                    m, s = scales[unit, side][1:]
                    sent[unit, side, 0:HEAD, :] = jnp.concatenate([m, s, jnp.zeros((HEAD - 2, HALF), F32)], axis=0)
                sent[unit, side, HEAD + piece * PART : HEAD + (piece + 1) * PART, :] = p
                ring_copy(unit, side, piece).start()

    top = first_chunk(0, None)
    for j in range(STREAMS):
        shares[j].wait_recv()
        prepare_landmarks(1, j)
    top = first_chunk(1, top)
    for block in range(2):
        inner(1, block)
    for group in groups:
        for j in group:
            finish(j)
        for j in group:
            prepare_landmarks(2, j)
    top = first_chunk(2, top)
    for j in range(STREAMS):
        shares[STREAMS + j].wait_recv()
        prepare_landmarks(3, j)
    first_chunk(3, top)
    handle(0)
    for block in range(2, BLOCKS):
        inner(1, block)

    for t in range(1, RING):
        total = mass = None
        for block in range(BLOCKS):
            if t + 1 < RING:
                inner(t + 1, block)
            total, mass = outer(t, block, total, mass, tops[t])
        held[t, 0:1, :] = tops[t]
        held[t, 1:2, :] = mass
        held[t, HEAD:, :] = total
        if t == 1:
            handle(1, (0,))
        elif t == 2:
            handle(1, (1,))
        elif t == 4:
            handle(2)
        elif t == 6:
            handle(3)
    for unit in range(4, UNITS):
        handle(unit)
    for piece in range(SUBS):
        for unit in (UNITS - 2, UNITS - 1):
            for side in range(2):
                ring_copy(unit, side, piece).wait_recv()
        for half in range(2):
            incoming = [(UNITS - 1 - half, 0), (UNITS - 2 + half, 1)]
            p = merge(half, piece, RING - 1, half, incoming) / scales[half][2]
            out_ref[lanes_of(half), piece * PART : (piece + 1) * PART] = p.T

    w_send.wait_send()
    for copy in copies + shares:
        copy.wait_send()
    for unit in range(UNITS):
        for side in range(2):
            for piece in range(SUBS):
                ring_copy(unit, side, piece).wait_send()


def shards(embeddings, landmark_index, cluster_weights):
    vmem = lambda *shape, dtype=F32: pltpu.VMEM(shape, dtype)
    dma = lambda *shape: pltpu.SemaphoreType.DMA(shape)
    return pl.pallas_call(
        kernel,
        out_shape=jax.ShapeDtypeStruct((CHUNK, C), F32),
        in_specs=[
            pl.BlockSpec(memory_space=pl.ANY),
            pl.BlockSpec(memory_space=pltpu.SMEM),
            pl.BlockSpec(memory_space=pl.ANY),
        ],
        out_specs=pl.BlockSpec(memory_space=pltpu.VMEM),
        scratch_shapes=[
            vmem(ROWS, D),
            vmem(OWN, D),
            vmem(PAIR, D),
            vmem(STREAMS, R // 2, D),
            vmem(STREAMS, R // 4, D),
            vmem(STREAMS, R // 4, D),
            vmem(STREAMS, R // 4, D),
            vmem(STREAMS, R // 2, D),
            vmem(STREAMS, R // 4, D),
            vmem(STREAMS, R // 4, D),
            vmem(PAIR, C),
            vmem(2 * C, PAIR, dtype=BF16),
            vmem(PAIR, 3 * D, dtype=BF16),
            vmem(PAIR, 128),
            vmem(RING, CHUNK, 3 * D, dtype=BF16),
            vmem(RING, 1, CHUNK),
            vmem(PAIR, CHUNK),
            vmem(PAIR, CHUNK),
            vmem(RING, MSG, CHUNK),
            vmem(UNITS, 2, MSG, HALF),
            vmem(UNITS, 2, MSG, HALF),
            dma(LOADS),
            pltpu.SemaphoreType.DMA,
            dma(6, STREAMS),
            dma(6, STREAMS),
            dma(2 * STREAMS),
            dma(2 * STREAMS),
            pltpu.SemaphoreType.DMA,
            pltpu.SemaphoreType.DMA,
            dma(UNITS, 2, SUBS),
            dma(UNITS, 2, SUBS),
        ],
        compiler_params=pltpu.CompilerParams(
            collective_id=0, has_side_effects=True, vmem_limit_bytes=56 * 2**20
        ),
    )(embeddings, landmark_index, cluster_weights)


def solution(mesh):
    return jax.shard_map(
        shards,
        mesh=mesh,
        in_specs=(P("sample", None), P("landmark"), P("landmark", None)),
        out_specs=P(("sample", "landmark"), None),
        check_vma=False,
    )
```

```python
import jax
import jax.numpy as jnp
from jax import lax
from jax.experimental import pallas as pl
from jax.experimental.pallas import tpu as pltpu
from jax.sharding import PartitionSpec as P

MESH = pl.DeviceIdType.MESH
F32 = jnp.float32
BF16 = jnp.bfloat16

D = 512
C = 256
ROWS = 4096
OWN = 512
PAIR = 2 * OWN
RING = 8
CHUNK = 256
HALF = CHUNK // 2
STREAMS = 8
R = OWN // STREAMS
HEAD = 8
MSG = HEAD + C
SUBS = 2
PART = C // SUBS
BLOCKS = 4
BLOCK = PAIR // BLOCKS
LOADS = 8
ORDER = (4, 3, -3, 2, -2, 1, -1, 0)
UNITS = RING - 1


def split(a):
    hi = a.astype(BF16)
    return hi, (a - hi.astype(F32)).astype(BF16)


def kernel(
    emb_hbm, idx_ref, w_hbm, out_ref,
    emb, pick, land, buf0, buf1, buf2, buf3, acc1, acc2, acc3,
    wts, ww, ll, lsq2, xx, xsq2, dots0, dots1, held, sent, got,
    load_sem, w_sem, send_sem, recv_sem, sib_send, sib_recv, ws_send, ws_recv, ring_send, ring_recv,
):
    sample = lax.axis_index("sample")
    mark = lax.axis_index("landmark")
    x, y = sample // 4, sample % 4
    z, core = mark // 2, mark % 2

    partners = [
        ((x + 1 - 2 * (x % 2)) * 4 + y, mark),
        ((3 - x) * 4 + y, mark),
        (x * 4 + y + 1 - 2 * (y % 2), mark),
        (x * 4 + 3 - y, mark),
    ]
    bits = [(x % 2 + x // 2) % 2, x // 2, (y % 2 + y // 2) % 2, y // 2]
    sibling = (sample, z * 2 + 1 - core)
    above = (sample, ((z + 1) % RING) * 2 + core)
    below = (sample, ((z + RING - 1) % RING) * 2 + core)

    loads = []
    for i in range(LOADS):
        part = pl.ds(i * (ROWS // LOADS), ROWS // LOADS)
        load = pltpu.make_async_copy(emb_hbm.at[part], emb.at[part], load_sem.at[i])
        load.start()
        loads.append(load)
    own_w = pl.ds(pl.multiple_of(core * OWN, OWN), OWN)
    w_load = pltpu.make_async_copy(w_hbm, wts.at[own_w], w_sem)
    w_load.start()

    barrier = pltpu.get_barrier_semaphore()
    for other in partners + [sibling, above, below]:
        pl.semaphore_signal(barrier, inc=1, device_id=other, device_id_type=MESH)

    first = sample * ROWS

    def pick_rows(start, count):
        def some(i, carry):
            for u in range(32):
                row = start + i * 32 + u
                place = idx_ref[row] - first
                owned = jnp.logical_and(place >= 0, place < ROWS)
                found = emb[pl.ds(jnp.clip(place, 0, ROWS - 1), 1), :]
                pick[pl.ds(row, 1), :] = jnp.where(owned, found, 0.0)
            return carry

        lax.fori_loop(0, count // 32, some, 0)

    def prepare(t):
        chip = (z + RING + ORDER[t]) % RING
        rows = emb[pl.ds(pl.multiple_of((chip * 2 + core) * CHUNK, CHUNK), CHUNK), :]
        hi, lo = split(4.0 * rows)
        xx[t, :, 0:D] = hi
        xx[t, :, D : 2 * D] = lo
        xx[t, :, 2 * D :] = hi
        sq = rows * rows
        sq = (sq[:, 0:128] + sq[:, 128:256]) + (sq[:, 256:384] + sq[:, 384:512])
        xsq2[t] = 2.0 * jnp.sum(sq.T, axis=0, keepdims=True)

    base = core * OWN
    other_base = (1 - core) * OWN

    def rows_at(start, count):
        return pl.ds(pl.multiple_of(start, 8), count)

    def block_rows(block, j):
        b0 = bits[j % 4]
        late = block // 2
        half = b0 + late - 2 * b0 * late
        return (base if block % 2 == 0 else other_base) + j * R + half * (R // 2)

    def prepare_landmarks(block, j):
        rows = land[rows_at(block_rows(block, j), R // 2), :]
        hi, lo = split(rows)
        here = pl.ds(block * BLOCK + j * (R // 2), R // 2)
        ll[here, 0:D] = hi
        ll[here, D : 2 * D] = hi
        ll[here, 2 * D :] = lo
        lsq2[here, :] = jnp.broadcast_to(2.0 * jnp.sum(rows * rows, axis=1, keepdims=True), (R // 2, 128))

    def prepare_weights(block):
        rows = [wts[rows_at(block_rows(block, j), R // 2), :] for j in range(STREAMS)]
        hi, lo = split(jnp.concatenate(rows, axis=0).T)
        here = slice(block * BLOCK, (block + 1) * BLOCK)
        ww[0:C, here] = hi
        ww[C:, here] = lo

    copies = []

    def send(step, j, src, dst, dim):
        copy = pltpu.make_async_remote_copy(
            src, dst, send_sem.at[step, j], recv_sem.at[step, j],
            device_id=partners[dim], device_id_type=MESH,
        )
        copy.start()
        copies.append(copy)
        return copy

    groups = [range(g, g + 4) for g in range(0, STREAMS, 4)]
    flight = [None] * STREAMS
    shares = [None] * (2 * STREAMS)

    def pick_half(j, half):
        pick_rows(j * R + half * (R // 2), R // 2)

    def halve_first(j):
        b0 = bits[j % 4]
        flight[j] = send(0, j, pick.at[rows_at(j * R + (1 - b0) * (R // 2), R // 2)], buf0.at[j], j % 4)

    def halve_second(j):
        b0, b1 = bits[j % 4], bits[(j + 1) % 4]
        flight[j].wait_recv()
        acc1[j] = pick[rows_at(j * R + b0 * (R // 2), R // 2), :] + buf0[j]
        flight[j] = send(1, j, acc1.at[j, rows_at((1 - b1) * (R // 4), R // 4)], buf1.at[j], (j + 1) % 4)

    def exchange_first(j):
        b1 = bits[(j + 1) % 4]
        flight[j].wait_recv()
        acc2[j] = acc1[j, rows_at(b1 * (R // 4), R // 4), :] + buf1[j]
        flight[j] = send(2, j, acc2.at[j], buf2.at[j], (j + 2) % 4)

    def exchange_second(j):
        flight[j].wait_recv()
        acc3[j] = acc2[j] + buf2[j]
        flight[j] = send(3, j, acc3.at[j], buf3.at[j], (j + 3) % 4)

    def gather_first(j):
        b0, b1 = bits[j % 4], bits[(j + 1) % 4]
        here = rows_at(base + j * R + b0 * (R // 2) + b1 * (R // 4), R // 4)
        flight[j].wait_recv()
        land[here, :] = acc3[j] + buf3[j]
        flight[j] = send(4, j, land.at[here], land.at[here], (j + 1) % 4)

    def share(which, start, count):
        here = rows_at(start, count)
        copy = pltpu.make_async_remote_copy(
            land.at[here], land.at[here], sib_send.at[which], sib_recv.at[which],
            device_id=sibling, device_id_type=MESH,
        )
        copy.start()
        shares[which] = copy

    def gather_second(j):
        here = rows_at(block_rows(0, j), R // 2)
        flight[j].wait_recv()
        flight[j] = send(5, j, land.at[here], land.at[here], j % 4)
        share(j, block_rows(0, j), R // 2)

    def finish(j):
        flight[j].wait_recv()
        share(STREAMS + j, block_rows(2, j), R // 2)

    for load in loads:
        load.wait()
    pl.semaphore_wait(barrier, 7)
    for j in range(STREAMS):
        pick_half(j, 1 - bits[j % 4])
        halve_first(j)
    w_load.wait()
    w_send = pltpu.make_async_remote_copy(
        wts.at[own_w], wts.at[own_w], ws_send, ws_recv, device_id=sibling, device_id_type=MESH
    )
    w_send.start()
    for j in range(STREAMS):
        pick_half(j, bits[j % 4])
    fillers = [
        lambda: (prepare(0), prepare(1), prepare(2)),
        lambda: (prepare(3), prepare(4), prepare(5)),
        lambda: (prepare(6), prepare(7)),
        lambda: (prepare_weights(0), prepare_weights(2)),
        lambda: (w_send.wait_recv(), prepare_weights(1), prepare_weights(3)),
    ]
    for stage in (halve_second, exchange_first, exchange_second, gather_first, gather_second):
        for group in groups:
            for j in group:
                stage(j)
            if fillers:
                fillers.pop(0)()
    for j in range(STREAMS):
        prepare_landmarks(0, j)

    dots = (dots0, dots1)
    tops = [None] * RING

    def inner(t, block):
        here = slice(block * BLOCK, (block + 1) * BLOCK)
        product = lax.dot_general(ll[here, :], xx[t], (((1,), (1,)), ((), ())), preferred_element_type=F32)
        both = lsq2[here, :]
        logits = product - jnp.concatenate([both, both], axis=1) - xsq2[t]
        dots[t % 2][here, :] = logits
        top = jnp.max(logits, axis=0, keepdims=True)
        tops[t] = top if tops[t] is None else jnp.maximum(tops[t], top)

    def outer(t, block, total, mass, top):
        here = slice(block * BLOCK, (block + 1) * BLOCK)
        weight = jnp.exp(dots[t % 2][here, :] - top)
        hi, lo = split(weight)
        part = jnp.dot(ww[:, here], hi, preferred_element_type=F32)
        part = part[:C] + part[C:] + jnp.dot(ww[0:C, here], lo, preferred_element_type=F32)
        here_mass = jnp.sum(weight, axis=0, keepdims=True)
        if total is None:
            return part, here_mass
        return total + part, mass + here_mass

    def first_chunk(block, old):
        inner(0, block)
        if block == 0:
            total, mass = outer(0, 0, None, None, tops[0])
        else:
            shrink = jnp.exp(old - tops[0])
            total, mass = outer(0, block, held[0, HEAD:, :] * shrink, held[0, 1:2, :] * shrink, tops[0])
        held[0, 0:1, :] = tops[0]
        held[0, 1:2, :] = mass
        held[0, HEAD:, :] = total
        return tops[0]

    def piece_rows(piece):
        return slice(0 if piece == 0 else HEAD + piece * PART, HEAD + (piece + 1) * PART)

    def ring_copy(unit, side, piece):
        here = piece_rows(piece)
        here = pl.ds(here.start, here.stop - here.start)
        return pltpu.make_async_remote_copy(
            sent.at[unit, side, here], got.at[unit, side, here],
            ring_send.at[unit, side, piece], ring_recv.at[unit, side, piece],
            device_id=above if side == 0 else below, device_id_type=MESH,
        )

    def lanes_of(half):
        return slice(half * HALF, (half + 1) * HALF)

    scales = {}

    def merge(key, piece, chunk, half, incoming):
        if piece == 0:
            m, s = held[chunk, 0:1, lanes_of(half)], held[chunk, 1:2, lanes_of(half)]
            factors = []
            if incoming:
                m_in = [got[u, side, 0:1, :] for u, side in incoming]
                top = m
                for other in m_in:
                    top = jnp.maximum(top, other)
                factors = [jnp.exp(other - top) for other in [m] + m_in]
                s = s * factors[0]
                for (u, side), factor in zip(incoming, factors[1:]):
                    s = s + got[u, side, 1:2, :] * factor
                m = top
            scales[key] = factors, m, s
        factors = scales[key][0]
        rows = slice(HEAD + piece * PART, HEAD + (piece + 1) * PART)
        p = held[chunk, rows, lanes_of(half)]
        if incoming:
            p = p * factors[0]
            for (u, side), factor in zip(incoming, factors[1:]):
                p = p + got[u, side, rows, :] * factor
        return p

    def handle(unit, sides=(0, 1)):
        hop = (unit + 1) // 2
        for piece in range(SUBS):
            for side in sides:
                incoming = []
                if unit >= 2:
                    ring_copy(unit - 2, side, piece).wait_recv()
                    incoming = [(unit - 2, side)]
                chunk = 0 if hop == 0 else 2 * hop - 1 + side
                half = (unit + side) % 2
                p = merge((unit, side), piece, chunk, half, incoming)
                if piece == 0:
                    m, s = scales[unit, side][1:]
                    sent[unit, side, 0:HEAD, :] = jnp.concatenate([m, s, jnp.zeros((HEAD - 2, HALF), F32)], axis=0)
                sent[unit, side, HEAD + piece * PART : HEAD + (piece + 1) * PART, :] = p
                ring_copy(unit, side, piece).start()

    top = first_chunk(0, None)
    for j in range(STREAMS):
        shares[j].wait_recv()
        prepare_landmarks(1, j)
    top = first_chunk(1, top)
    for block in range(2):
        inner(1, block)
    for group in groups:
        for j in group:
            finish(j)
        for j in group:
            prepare_landmarks(2, j)
    top = first_chunk(2, top)
    for j in range(STREAMS):
        shares[STREAMS + j].wait_recv()
        prepare_landmarks(3, j)
    first_chunk(3, top)
    handle(0)
    for block in range(2, BLOCKS):
        inner(1, block)

    for t in range(1, RING):
        total = mass = None
        for block in range(BLOCKS):
            if t + 1 < RING:
                inner(t + 1, block)
            total, mass = outer(t, block, total, mass, tops[t])
        held[t, 0:1, :] = tops[t]
        held[t, 1:2, :] = mass
        held[t, HEAD:, :] = total
        if t == 1:
            handle(1, (0,))
        elif t == 2:
            handle(1, (1,))
        elif t == 3:
            handle(2)
        elif t == 5:
            handle(3)
    for unit in range(4, UNITS):
        handle(unit)
    for piece in range(SUBS):
        for unit in (UNITS - 2, UNITS - 1):
            for side in range(2):
                ring_copy(unit, side, piece).wait_recv()
        for half in range(2):
            incoming = [(UNITS - 1 - half, 0), (UNITS - 2 + half, 1)]
            p = merge(half, piece, RING - 1, half, incoming) / scales[half][2]
            out_ref[lanes_of(half), piece * PART : (piece + 1) * PART] = p.T

    w_send.wait_send()
    for copy in copies + shares:
        copy.wait_send()
    for unit in range(UNITS):
        for side in range(2):
            for piece in range(SUBS):
                ring_copy(unit, side, piece).wait_send()


def shards(embeddings, landmark_index, cluster_weights):
    vmem = lambda *shape, dtype=F32: pltpu.VMEM(shape, dtype)
    dma = lambda *shape: pltpu.SemaphoreType.DMA(shape)
    return pl.pallas_call(
        kernel,
        out_shape=jax.ShapeDtypeStruct((CHUNK, C), F32),
        in_specs=[
            pl.BlockSpec(memory_space=pl.ANY),
            pl.BlockSpec(memory_space=pltpu.SMEM),
            pl.BlockSpec(memory_space=pl.ANY),
        ],
        out_specs=pl.BlockSpec(memory_space=pltpu.VMEM),
        scratch_shapes=[
            vmem(ROWS, D),
            vmem(OWN, D),
            vmem(PAIR, D),
            vmem(STREAMS, R // 2, D),
            vmem(STREAMS, R // 4, D),
            vmem(STREAMS, R // 4, D),
            vmem(STREAMS, R // 4, D),
            vmem(STREAMS, R // 2, D),
            vmem(STREAMS, R // 4, D),
            vmem(STREAMS, R // 4, D),
            vmem(PAIR, C),
            vmem(2 * C, PAIR, dtype=BF16),
            vmem(PAIR, 3 * D, dtype=BF16),
            vmem(PAIR, 128),
            vmem(RING, CHUNK, 3 * D, dtype=BF16),
            vmem(RING, 1, CHUNK),
            vmem(PAIR, CHUNK),
            vmem(PAIR, CHUNK),
            vmem(RING, MSG, CHUNK),
            vmem(UNITS, 2, MSG, HALF),
            vmem(UNITS, 2, MSG, HALF),
            dma(LOADS),
            pltpu.SemaphoreType.DMA,
            dma(6, STREAMS),
            dma(6, STREAMS),
            dma(2 * STREAMS),
            dma(2 * STREAMS),
            pltpu.SemaphoreType.DMA,
            pltpu.SemaphoreType.DMA,
            dma(UNITS, 2, SUBS),
            dma(UNITS, 2, SUBS),
        ],
        compiler_params=pltpu.CompilerParams(
            collective_id=0, has_side_effects=True, vmem_limit_bytes=56 * 2**20
        ),
    )(embeddings, landmark_index, cluster_weights)


def solution(mesh):
    return jax.shard_map(
        shards,
        mesh=mesh,
        in_specs=(P("sample", None), P("landmark"), P("landmark", None)),
        out_specs=P(("sample", "landmark"), None),
        check_vma=False,
    )
```

```python
import jax
import jax.numpy as jnp
from jax import lax
from jax.experimental import pallas as pl
from jax.experimental.pallas import tpu as pltpu
from jax.sharding import PartitionSpec as P

MESH = pl.DeviceIdType.MESH
F32 = jnp.float32
BF16 = jnp.bfloat16

D = 512
C = 256
ROWS = 4096
OWN = 512
PAIR = 2 * OWN
RING = 8
CHUNK = 256
HALF = CHUNK // 2
STREAMS = 8
R = OWN // STREAMS
HEAD = 8
MSG = HEAD + C
SUBS = 1
PART = C // SUBS
BLOCKS = 4
BLOCK = PAIR // BLOCKS
LOADS = 8
ORDER = (4, 3, -3, 2, -2, 1, -1, 0)
UNITS = RING - 1


def split(a):
    hi = a.astype(BF16)
    return hi, (a - hi.astype(F32)).astype(BF16)


def kernel(
    emb_hbm, idx_ref, w_hbm, out_ref,
    emb, pick, land, buf0, buf1, buf2, buf3, acc1, acc2, acc3,
    wts, ww, ll, lsq2, xx, xsq2, dots0, dots1, held, sent, got,
    load_sem, w_sem, send_sem, recv_sem, sib_send, sib_recv, ws_send, ws_recv, ring_send, ring_recv,
):
    sample = lax.axis_index("sample")
    mark = lax.axis_index("landmark")
    x, y = sample // 4, sample % 4
    z, core = mark // 2, mark % 2

    partners = [
        ((x + 1 - 2 * (x % 2)) * 4 + y, mark),
        ((3 - x) * 4 + y, mark),
        (x * 4 + y + 1 - 2 * (y % 2), mark),
        (x * 4 + 3 - y, mark),
    ]
    bits = [(x % 2 + x // 2) % 2, x // 2, (y % 2 + y // 2) % 2, y // 2]
    sibling = (sample, z * 2 + 1 - core)
    above = (sample, ((z + 1) % RING) * 2 + core)
    below = (sample, ((z + RING - 1) % RING) * 2 + core)

    loads = []
    for i in range(LOADS):
        part = pl.ds(i * (ROWS // LOADS), ROWS // LOADS)
        load = pltpu.make_async_copy(emb_hbm.at[part], emb.at[part], load_sem.at[i])
        load.start()
        loads.append(load)
    own_w = pl.ds(pl.multiple_of(core * OWN, OWN), OWN)
    w_load = pltpu.make_async_copy(w_hbm, wts.at[own_w], w_sem)
    w_load.start()

    barrier = pltpu.get_barrier_semaphore()
    for other in partners + [sibling, above, below]:
        pl.semaphore_signal(barrier, inc=1, device_id=other, device_id_type=MESH)

    first = sample * ROWS

    def pick_rows(start, count):
        def some(i, carry):
            for u in range(32):
                row = start + i * 32 + u
                place = idx_ref[row] - first
                owned = jnp.logical_and(place >= 0, place < ROWS)
                found = emb[pl.ds(jnp.clip(place, 0, ROWS - 1), 1), :]
                pick[pl.ds(row, 1), :] = jnp.where(owned, found, 0.0)
            return carry

        lax.fori_loop(0, count // 32, some, 0)

    def prepare(t):
        chip = (z + RING + ORDER[t]) % RING
        rows = emb[pl.ds(pl.multiple_of((chip * 2 + core) * CHUNK, CHUNK), CHUNK), :]
        hi, lo = split(4.0 * rows)
        xx[t, :, 0:D] = hi
        xx[t, :, D : 2 * D] = lo
        xx[t, :, 2 * D :] = hi
        sq = rows * rows
        sq = (sq[:, 0:128] + sq[:, 128:256]) + (sq[:, 256:384] + sq[:, 384:512])
        xsq2[t] = 2.0 * jnp.sum(sq.T, axis=0, keepdims=True)

    base = core * OWN
    other_base = (1 - core) * OWN

    def rows_at(start, count):
        return pl.ds(pl.multiple_of(start, 8), count)

    def block_rows(block, j):
        b0 = bits[j % 4]
        late = block // 2
        half = b0 + late - 2 * b0 * late
        return (base if block % 2 == 0 else other_base) + j * R + half * (R // 2)

    def prepare_landmarks(block, j):
        rows = land[rows_at(block_rows(block, j), R // 2), :]
        hi, lo = split(rows)
        here = pl.ds(block * BLOCK + j * (R // 2), R // 2)
        ll[here, 0:D] = hi
        ll[here, D : 2 * D] = hi
        ll[here, 2 * D :] = lo
        lsq2[here, :] = jnp.broadcast_to(2.0 * jnp.sum(rows * rows, axis=1, keepdims=True), (R // 2, 128))

    def prepare_weights(block):
        rows = [wts[rows_at(block_rows(block, j), R // 2), :] for j in range(STREAMS)]
        hi, lo = split(jnp.concatenate(rows, axis=0).T)
        here = slice(block * BLOCK, (block + 1) * BLOCK)
        ww[0:C, here] = hi
        ww[C:, here] = lo

    copies = []

    def send(step, j, src, dst, dim):
        copy = pltpu.make_async_remote_copy(
            src, dst, send_sem.at[step, j], recv_sem.at[step, j],
            device_id=partners[dim], device_id_type=MESH,
        )
        copy.start()
        copies.append(copy)
        return copy

    groups = [range(g, g + 4) for g in range(0, STREAMS, 4)]
    flight = [None] * STREAMS
    shares = [None] * (2 * STREAMS)

    def pick_half(j, half):
        pick_rows(j * R + half * (R // 2), R // 2)

    def halve_first(j):
        b0 = bits[j % 4]
        flight[j] = send(0, j, pick.at[rows_at(j * R + (1 - b0) * (R // 2), R // 2)], buf0.at[j], j % 4)

    def halve_second(j):
        b0, b1 = bits[j % 4], bits[(j + 1) % 4]
        flight[j].wait_recv()
        acc1[j] = pick[rows_at(j * R + b0 * (R // 2), R // 2), :] + buf0[j]
        flight[j] = send(1, j, acc1.at[j, rows_at((1 - b1) * (R // 4), R // 4)], buf1.at[j], (j + 1) % 4)

    def exchange_first(j):
        b1 = bits[(j + 1) % 4]
        flight[j].wait_recv()
        acc2[j] = acc1[j, rows_at(b1 * (R // 4), R // 4), :] + buf1[j]
        flight[j] = send(2, j, acc2.at[j], buf2.at[j], (j + 2) % 4)

    def exchange_second(j):
        flight[j].wait_recv()
        acc3[j] = acc2[j] + buf2[j]
        flight[j] = send(3, j, acc3.at[j], buf3.at[j], (j + 3) % 4)

    def gather_first(j):
        b0, b1 = bits[j % 4], bits[(j + 1) % 4]
        here = rows_at(base + j * R + b0 * (R // 2) + b1 * (R // 4), R // 4)
        flight[j].wait_recv()
        land[here, :] = acc3[j] + buf3[j]
        flight[j] = send(4, j, land.at[here], land.at[here], (j + 1) % 4)

    def share(which, start, count):
        here = rows_at(start, count)
        copy = pltpu.make_async_remote_copy(
            land.at[here], land.at[here], sib_send.at[which], sib_recv.at[which],
            device_id=sibling, device_id_type=MESH,
        )
        copy.start()
        shares[which] = copy

    def gather_second(j):
        here = rows_at(block_rows(0, j), R // 2)
        flight[j].wait_recv()
        flight[j] = send(5, j, land.at[here], land.at[here], j % 4)
        share(j, block_rows(0, j), R // 2)

    def finish(j):
        flight[j].wait_recv()
        share(STREAMS + j, block_rows(2, j), R // 2)

    for load in loads:
        load.wait()
    pl.semaphore_wait(barrier, 7)
    for j in range(STREAMS):
        pick_half(j, 1 - bits[j % 4])
        halve_first(j)
    w_load.wait()
    w_send = pltpu.make_async_remote_copy(
        wts.at[own_w], wts.at[own_w], ws_send, ws_recv, device_id=sibling, device_id_type=MESH
    )
    w_send.start()
    for j in range(STREAMS):
        pick_half(j, bits[j % 4])
    fillers = [
        lambda: (prepare(0), prepare(1), prepare(2)),
        lambda: (prepare(3), prepare(4), prepare(5)),
        lambda: (prepare(6), prepare(7)),
        lambda: (prepare_weights(0), prepare_weights(2)),
        lambda: (w_send.wait_recv(), prepare_weights(1), prepare_weights(3)),
    ]
    for stage in (halve_second, exchange_first, exchange_second, gather_first, gather_second):
        for group in groups:
            for j in group:
                stage(j)
            if fillers:
                fillers.pop(0)()
    for j in range(STREAMS):
        prepare_landmarks(0, j)

    dots = (dots0, dots1)
    tops = [None] * RING

    def inner(t, block):
        here = slice(block * BLOCK, (block + 1) * BLOCK)
        product = lax.dot_general(ll[here, :], xx[t], (((1,), (1,)), ((), ())), preferred_element_type=F32)
        both = lsq2[here, :]
        logits = product - jnp.concatenate([both, both], axis=1) - xsq2[t]
        dots[t % 2][here, :] = logits
        top = jnp.max(logits, axis=0, keepdims=True)
        tops[t] = top if tops[t] is None else jnp.maximum(tops[t], top)

    def outer(t, block, total, mass, top):
        here = slice(block * BLOCK, (block + 1) * BLOCK)
        weight = jnp.exp(dots[t % 2][here, :] - top)
        hi, lo = split(weight)
        part = jnp.dot(ww[:, here], hi, preferred_element_type=F32)
        part = part[:C] + part[C:] + jnp.dot(ww[0:C, here], lo, preferred_element_type=F32)
        here_mass = jnp.sum(weight, axis=0, keepdims=True)
        if total is None:
            return part, here_mass
        return total + part, mass + here_mass

    def first_chunk(block, old):
        inner(0, block)
        if block == 0:
            total, mass = outer(0, 0, None, None, tops[0])
        else:
            shrink = jnp.exp(old - tops[0])
            total, mass = outer(0, block, held[0, HEAD:, :] * shrink, held[0, 1:2, :] * shrink, tops[0])
        held[0, 0:1, :] = tops[0]
        held[0, 1:2, :] = mass
        held[0, HEAD:, :] = total
        return tops[0]

    def piece_rows(piece):
        return slice(0 if piece == 0 else HEAD + piece * PART, HEAD + (piece + 1) * PART)

    def ring_copy(unit, side, piece):
        here = piece_rows(piece)
        here = pl.ds(here.start, here.stop - here.start)
        return pltpu.make_async_remote_copy(
            sent.at[unit, side, here], got.at[unit, side, here],
            ring_send.at[unit, side, piece], ring_recv.at[unit, side, piece],
            device_id=above if side == 0 else below, device_id_type=MESH,
        )

    def lanes_of(half):
        return slice(half * HALF, (half + 1) * HALF)

    scales = {}

    def merge(key, piece, chunk, half, incoming):
        if piece == 0:
            m, s = held[chunk, 0:1, lanes_of(half)], held[chunk, 1:2, lanes_of(half)]
            factors = []
            if incoming:
                m_in = [got[u, side, 0:1, :] for u, side in incoming]
                top = m
                for other in m_in:
                    top = jnp.maximum(top, other)
                factors = [jnp.exp(other - top) for other in [m] + m_in]
                s = s * factors[0]
                for (u, side), factor in zip(incoming, factors[1:]):
                    s = s + got[u, side, 1:2, :] * factor
                m = top
            scales[key] = factors, m, s
        factors = scales[key][0]
        rows = slice(HEAD + piece * PART, HEAD + (piece + 1) * PART)
        p = held[chunk, rows, lanes_of(half)]
        if incoming:
            p = p * factors[0]
            for (u, side), factor in zip(incoming, factors[1:]):
                p = p + got[u, side, rows, :] * factor
        return p

    def handle(unit, sides=(0, 1)):
        hop = (unit + 1) // 2
        for piece in range(SUBS):
            for side in sides:
                incoming = []
                if unit >= 2:
                    ring_copy(unit - 2, side, piece).wait_recv()
                    incoming = [(unit - 2, side)]
                chunk = 0 if hop == 0 else 2 * hop - 1 + side
                half = (unit + side) % 2
                p = merge((unit, side), piece, chunk, half, incoming)
                if piece == 0:
                    m, s = scales[unit, side][1:]
                    sent[unit, side, 0:HEAD, :] = jnp.concatenate([m, s, jnp.zeros((HEAD - 2, HALF), F32)], axis=0)
                sent[unit, side, HEAD + piece * PART : HEAD + (piece + 1) * PART, :] = p
                ring_copy(unit, side, piece).start()

    top = first_chunk(0, None)
    for j in range(STREAMS):
        shares[j].wait_recv()
        prepare_landmarks(1, j)
    top = first_chunk(1, top)
    for block in range(2):
        inner(1, block)
    for group in groups:
        for j in group:
            finish(j)
        for j in group:
            prepare_landmarks(2, j)
    top = first_chunk(2, top)
    for j in range(STREAMS):
        shares[STREAMS + j].wait_recv()
        prepare_landmarks(3, j)
    first_chunk(3, top)
    handle(0)
    for block in range(2, BLOCKS):
        inner(1, block)

    for t in range(1, RING):
        total = mass = None
        for block in range(BLOCKS):
            if t + 1 < RING:
                inner(t + 1, block)
            total, mass = outer(t, block, total, mass, tops[t])
        held[t, 0:1, :] = tops[t]
        held[t, 1:2, :] = mass
        held[t, HEAD:, :] = total
        if t == 1:
            handle(1, (0,))
        elif t == 2:
            handle(1, (1,))
        elif t == 3:
            handle(2)
        elif t == 5:
            handle(3)
    for unit in range(4, UNITS):
        handle(unit)
    for piece in range(SUBS):
        for unit in (UNITS - 2, UNITS - 1):
            for side in range(2):
                ring_copy(unit, side, piece).wait_recv()
        for half in range(2):
            incoming = [(UNITS - 1 - half, 0), (UNITS - 2 + half, 1)]
            p = merge(half, piece, RING - 1, half, incoming) / scales[half][2]
            out_ref[lanes_of(half), piece * PART : (piece + 1) * PART] = p.T

    w_send.wait_send()
    for copy in copies + shares:
        copy.wait_send()
    for unit in range(UNITS):
        for side in range(2):
            for piece in range(SUBS):
                ring_copy(unit, side, piece).wait_send()


def shards(embeddings, landmark_index, cluster_weights):
    vmem = lambda *shape, dtype=F32: pltpu.VMEM(shape, dtype)
    dma = lambda *shape: pltpu.SemaphoreType.DMA(shape)
    return pl.pallas_call(
        kernel,
        out_shape=jax.ShapeDtypeStruct((CHUNK, C), F32),
        in_specs=[
            pl.BlockSpec(memory_space=pl.ANY),
            pl.BlockSpec(memory_space=pltpu.SMEM),
            pl.BlockSpec(memory_space=pl.ANY),
        ],
        out_specs=pl.BlockSpec(memory_space=pltpu.VMEM),
        scratch_shapes=[
            vmem(ROWS, D),
            vmem(OWN, D),
            vmem(PAIR, D),
            vmem(STREAMS, R // 2, D),
            vmem(STREAMS, R // 4, D),
            vmem(STREAMS, R // 4, D),
            vmem(STREAMS, R // 4, D),
            vmem(STREAMS, R // 2, D),
            vmem(STREAMS, R // 4, D),
            vmem(STREAMS, R // 4, D),
            vmem(PAIR, C),
            vmem(2 * C, PAIR, dtype=BF16),
            vmem(PAIR, 3 * D, dtype=BF16),
            vmem(PAIR, 128),
            vmem(RING, CHUNK, 3 * D, dtype=BF16),
            vmem(RING, 1, CHUNK),
            vmem(PAIR, CHUNK),
            vmem(PAIR, CHUNK),
            vmem(RING, MSG, CHUNK),
            vmem(UNITS, 2, MSG, HALF),
            vmem(UNITS, 2, MSG, HALF),
            dma(LOADS),
            pltpu.SemaphoreType.DMA,
            dma(6, STREAMS),
            dma(6, STREAMS),
            dma(2 * STREAMS),
            dma(2 * STREAMS),
            pltpu.SemaphoreType.DMA,
            pltpu.SemaphoreType.DMA,
            dma(UNITS, 2, SUBS),
            dma(UNITS, 2, SUBS),
        ],
        compiler_params=pltpu.CompilerParams(
            collective_id=0, has_side_effects=True, vmem_limit_bytes=56 * 2**20
        ),
    )(embeddings, landmark_index, cluster_weights)


def solution(mesh):
    return jax.shard_map(
        shards,
        mesh=mesh,
        in_specs=(P("sample", None), P("landmark"), P("landmark", None)),
        out_specs=P(("sample", "landmark"), None),
        check_vma=False,
    )
```
